256 devices in a mesh: row: 8 (over z_hi, x), col: 32 (over z_lo, y, core).
Axes of the slice: x: 4, y: 4, z: 8 (z_hi: 2, z_lo: 4; z = z_hi * 4 + z_lo), core: 2. Of those that a mesh axis runs over, the one named last changes fastest.
Arguments:
- features: bfloat16 [384, 512], P('col'), may hold values from -6 to 6
- weights: bfloat16 [1507328, 512], P(('row', 'col')), may hold values from -0.25 to 0.25
- label_bias: float32 [1507328], P(('row', 'col')), may hold values from -11 to -7
- pos_ids: int32 [384, 32], P('col'), may hold values from 0 to 1507327, as said below
- pos_count: int32 [384], P('col'), may hold values from 1 to 32
Outputs:
- weight_grad: bfloat16 [1507328, 512], P(('row', 'col'))
- bias_grad: float32 [1507328], P(('row', 'col'))
- feature_grad: bfloat16 [384, 512], P('col', 'row')
The draws below stay inside these ranges and needn't reach their ends.
Inputs may be any that keep to these rules, and one draw needn't show every extreme that they name: `pos_ids`: slots at or beyond an example's count are ignored; an id may repeat within one list.
All inputs are finite; a program needn't handle non-finite values.
Results may differ from the reference program's by a relative error of at most 0.0046.
Values may be sent and summed in bfloat16 or wider, within the bound.
No kernel may reach another device: no remote copies, remote signals or barrier semaphores. Data moves between devices by JAX's collectives and lax.ppermute only.
A program may use at most 128 MiB of HBM per device.

```python
import jax
import jax.numpy as jnp
from jax import lax

D = 512
LAB_DEV = 5888
NPOS = 32
B = 384
LABELS = 1507328


def shared_counts(key):
    count_key, spot_key, other_key = jax.random.split(key, 3)
    counts = jax.random.randint(count_key, (B,), 1, NPOS + 1, dtype=jnp.int32)
    full_row = jax.random.randint(spot_key, (), 0, B, dtype=jnp.int32)
    single_row = (full_row + 1 + jax.random.randint(other_key, (), 0, B - 1, dtype=jnp.int32)) % B
    row_index = jnp.arange(B, dtype=jnp.int32)
    counts = jnp.where(row_index == full_row, NPOS, counts)
    counts = jnp.where(row_index == single_row, 1, counts)
    return (counts.astype(jnp.int32), full_row)


def draw_pos_count(key, part):
    counts, full_row = shared_counts(key)
    return counts


def draw_pos_ids(key, part):
    counts, full_row = shared_counts(key)
    key = jax.random.fold_in(key, 5)
    id_key, pick_key, later_key, earlier_key = jax.random.split(key, 4)
    label_ids = jax.random.randint(id_key, (B, NPOS), 0, LABELS, dtype=jnp.int32)
    row_index = jnp.arange(B, dtype=jnp.int32)
    chosen = (jax.random.randint(pick_key, (B,), 0, 2, dtype=jnp.int32) == 0) | (row_index == full_row)
    chosen = chosen & (counts >= 2)
    later = 1 + jax.random.randint(later_key, (B,), 0, jnp.maximum(counts - 1, 1), dtype=jnp.int32)
    earlier = jax.random.randint(earlier_key, (B,), 0, later, dtype=jnp.int32)
    source = jnp.take_along_axis(label_ids, earlier[:, None], axis=1)
    slot_index = jnp.arange(NPOS, dtype=jnp.int32)
    replace = chosen[:, None] & (slot_index[None, :] == later[:, None])
    return jnp.where(replace, source, label_ids).astype(jnp.int32)


def levels(key, dims, pieces, least, high):
    loudness = 1.0
    for position, blocks in pieces:
        steps = jax.random.uniform(jax.random.fold_in(jax.random.fold_in(key, 6), position), (blocks,), jnp.float32, least / len(pieces), high / len(pieces))
        loudness = loudness * jnp.repeat(jnp.exp(steps), dims[position] // blocks).reshape((-1,) + (1,) * (len(dims) - 1 - position))
    return loudness


def gaussian(own_key, shape, scale, reach, cuts=(), held_as=jnp.bfloat16):
    entries = jax.random.normal(own_key, shape, jnp.float32) * scale
    if len(cuts) > 0:
        entries = levels(own_key, shape, cuts, -0.22, 0.18) * entries
    return jnp.clip(entries, min=-reach, max=reach).astype(held_as)


def setup_inputs(seed: int = 0) -> dict:
    arg_keys = jax.random.split(jax.random.key(seed), 6)
    features = gaussian(arg_keys[0], (B, D), 1.0, 6.0, ((0, 32),))
    weights = gaussian(arg_keys[1], (LABELS, D), D ** -0.5, 0.25, ((0, 256),))
    label_bias = jnp.clip(-11.0 + 4.0 * jax.random.uniform(arg_keys[2], (LABELS,), jnp.float32) ** levels(arg_keys[2], (LABELS,), ((0, 256),), -0.2, 0.2), -11.0, -7.0)
    pos_ids = draw_pos_ids(jax.random.fold_in(arg_keys[5], 71), 0)
    pos_count = draw_pos_count(jax.random.fold_in(arg_keys[5], 71), 0)
    return dict(features=features, weights=weights, label_bias=label_bias, pos_ids=pos_ids, pos_count=pos_count)


def block_grad(feat_rows, w_block, b_block, label_ids, live_slot, row_index, offset):
    logits = lax.dot_general(feat_rows, w_block, (((1,), (1,)), ((), ())), preferred_element_type=jnp.float32)
    logits = logits + b_block[None, :]
    lab_width = w_block.shape[0]
    local_ids = label_ids - offset
    inside = live_slot & (local_ids >= 0) & (local_ids < lab_width)
    target = jnp.where(inside, local_ids, lab_width).astype(jnp.int32)
    hit_table = jnp.zeros((feat_rows.shape[0], lab_width), jnp.float32).at[row_index, target].max(1.0, mode='drop')
    return (jax.nn.sigmoid(logits) - hit_table).astype(jnp.bfloat16)

def reference(features, weights, label_bias, pos_ids, pos_count):
    num_blocks = LABELS // LAB_DEV
    w_blocks = weights.reshape(num_blocks, LAB_DEV, D)
    b_blocks = label_bias.reshape(num_blocks, LAB_DEV)
    slot_index = jnp.arange(NPOS, dtype=jnp.int32)
    live_slot = slot_index[None, :] < pos_count[:, None]
    row_index = jnp.broadcast_to(jnp.arange(B, dtype=jnp.int32)[:, None], (B, NPOS))

    def scan_step(dx_carry, scan_item):
        w_block, b_block, block_index = scan_item
        offset = (block_index * LAB_DEV).astype(jnp.int32)
        label_grad = block_grad(features, w_block, b_block, pos_ids, live_slot, row_index, offset)
        dx_carry = dx_carry + jnp.dot(label_grad, w_block, preferred_element_type=jnp.float32)
        w_grad = lax.dot_general(label_grad, features, (((0,), (0,)), ((), ())), preferred_element_type=jnp.float32)
        b_grad = lax.optimization_barrier(jnp.sum(label_grad, axis=0, dtype=jnp.float32))
        return (dx_carry, (w_grad.astype(jnp.bfloat16), b_grad))
    dx_total, (w_grads, b_grads) = lax.scan(scan_step, jnp.zeros((B, D), jnp.float32), (w_blocks, b_blocks, jnp.arange(num_blocks, dtype=jnp.int32)))
    return (w_grads.reshape(LABELS, D), b_grads.reshape(LABELS), dx_total.astype(jnp.bfloat16))
```

```python
import functools

import jax
import jax.numpy as jnp
from jax import lax
from jax.experimental import pallas as pl
from jax.experimental.pallas import tpu as pltpu
from jax.sharding import Mesh, PartitionSpec as P

BF = jnp.bfloat16
F32 = jnp.float32
TILE = 256
KEY = 8192.0


def xor_permute(x, axis, size, bit):
    return lax.ppermute(x, axis, [(i, i ^ bit) for i in range(size)])


def grad_kernel(where_ref, own_ref, other_ref, w_hbm, bias_ref, g_ref, mine_ref, theirs_ref,
                f_scr, w_scr, first_scr, key_scr, dx_scr, sems):
    labels = w_scr.shape[0]
    tiles = labels // TILE
    half = own_ref.shape[0]
    rows = 2 * half
    width = f_scr.shape[1]

    def w_copy(t):
        at = pl.ds(t * TILE, TILE)
        return pltpu.make_async_copy(w_hbm.at[at], w_scr.at[at], sems.at[t])

    for t in range(tiles):
        w_copy(t).start()
    f_scr[0:half] = own_ref[:, 0:width]
    f_scr[half:rows] = other_ref[:, 0:width]

    digit = lax.broadcasted_iota(jnp.int32, (128, 128), 0)
    lane = lax.broadcasted_iota(jnp.int32, (128, 128), 1)
    same = (digit % 32) == (lane % 32)
    power = jnp.where(digit < 32, 1.0, jnp.where(digit < 64, 256.0, jnp.where(digit < 96, 65536.0, 0.0)))
    decode = jnp.where(same, power, 0.0).astype(BF)
    offset = where_ref[1].astype(F32)
    row = lax.broadcasted_iota(jnp.int32, (half, 128), 0).astype(F32)
    for h, ref in enumerate((own_ref, other_ref)):
        at = pl.ds(h * half, half)
        local = jnp.dot(ref[:, width:width + 128], decode, preferred_element_type=F32) - offset
        local = jnp.where((local >= 0.0) & (local < float(labels)), local, -1.0)
        first = jnp.max(local, axis=1, keepdims=True)
        first_scr[at] = jnp.broadcast_to(first, (half, 128))
        more = (local >= 0.0) & (local < first)
        key_scr[at] = jnp.where(more, (row + float(h * half)) * KEY + local, -1.0)
    dx_scr[...] = jnp.zeros_like(dx_scr)

    lanes = lax.broadcasted_iota(jnp.int32, (rows, 128), 1).astype(F32)

    def step(t, carry):
        w_copy(t).wait()
        at = pl.ds(pl.multiple_of(t * TILE, TILE), TILE)
        w = w_scr[at]
        logits = lax.dot_general(f_scr[...], w, (((1,), (1,)), ((), ())), preferred_element_type=F32)
        x = logits + bias_ref[:, at]
        s = 1.0 / (1.0 + jnp.exp(-x))
        base = (t * TILE).astype(F32)
        first = first_scr[...] - base
        hit = jnp.concatenate([lanes == first - 128.0 * k for k in range(TILE // 128)], axis=1)
        g = jnp.where(hit, s - 1.0, s).astype(BF)
        g_ref[:, at] = g
        dx_scr[...] += jnp.dot(g, w, preferred_element_type=F32)
        return carry

    lax.fori_loop(0, tiles, step, 0)

    def more_hits(top):
        return top >= 0.0

    def one_hit(top):
        k = top.astype(jnp.int32)
        b = k // int(KEY)
        l = k - b * int(KEY)
        b16 = pl.ds(pl.multiple_of((b // 16) * 16, 16), 16)
        l128 = pl.ds(pl.multiple_of((l // 128) * 128, 128), 128)
        r = lax.broadcasted_iota(jnp.int32, (16, 128), 0)
        c = lax.broadcasted_iota(jnp.int32, (16, 128), 1)
        spot = (r == b % 16) & (c == l % 128)
        old = g_ref[b16, l128].astype(F32)
        g_ref[b16, l128] = jnp.where(spot, old - 1.0, old).astype(BF)
        l16 = pl.ds(pl.multiple_of((l // 16) * 16, 16), 16)
        r = lax.broadcasted_iota(jnp.int32, (16, width), 0)
        w_row = jnp.sum(jnp.where(r == l % 16, w_scr[l16].astype(F32), 0.0), axis=0, keepdims=True)
        dx_scr[b16] -= jnp.where(r == b % 16, w_row, 0.0)
        keys = key_scr[...]
        keys = jnp.where(keys == top, -1.0, keys)
        key_scr[...] = keys
        return jnp.max(keys)

    lax.while_loop(more_hits, one_hit, jnp.max(key_scr[...]))

    me = where_ref[0]
    low = lax.broadcasted_iota(jnp.int32, (half, 128), 1) < 64
    per = mine_ref.shape[1]
    for h, ref in enumerate((mine_ref, theirs_ref)):
        at = pl.ds(h * half, half)
        for x in range(4):
            k = (x // 2) * 128
            left = dx_scr[at, k:k + 128]
            right = dx_scr[at, 256 + k:256 + k + 128]
            if x % 2 == 0:
                both = jnp.where(low, left, pltpu.roll(right, 64, 1))
            else:
                both = jnp.where(low, pltpu.roll(left, 64, 1), right)
            for j in range(16):
                ref[x * 16 + (me ^ j)] = both[j * per:(j + 1) * per].astype(ref.dtype)


def weight_kernel(g_ref, own_ref, other_ref, wg_ref, bg_ref):
    half = own_ref.shape[0]
    width = wg_ref.shape[1]
    g = g_ref[...]
    tn = (((0,), (0,)), ((), ()))
    acc = lax.dot_general(g[:half], own_ref[:, 0:width], tn, preferred_element_type=F32)
    acc += lax.dot_general(g[half:], other_ref[:, 0:width], tn, preferred_element_type=F32)
    wg_ref[...] = acc.astype(BF)
    bg_ref[...] = jnp.sum(g.astype(F32), axis=0, keepdims=True)


def local(features, weights, label_bias, pos_ids, pos_count):
    labels, width = weights.shape
    per, slots = pos_ids.shape
    half = per * 16
    rows = 2 * half
    slot = jnp.arange(slots, dtype=jnp.int32)
    ids = jnp.where(slot[None, :] < pos_count[:, None], pos_ids, 0xFFFFFF)
    pay = jnp.concatenate(
        [features, (ids & 255).astype(BF), ((ids >> 8) & 255).astype(BF), (ids >> 16).astype(BF),
         jnp.zeros((per, 32), BF)], axis=1)
    pay = jnp.concatenate([pay] + [xor_permute(pay, "y", 4, d) for d in (1, 2, 3)], axis=0)
    own = jnp.concatenate([pay] + [xor_permute(pay, "zl", 4, d) for d in (1, 2, 3)], axis=0)
    other = xor_permute(own, "c", 2, 1)

    zh, x, zl, y, c = (lax.axis_index(a) for a in ("zh", "x", "zl", "y", "c"))
    dev = (((zh * 4 + x) * 4 + zl) * 4 + y) * 2 + c
    where = jnp.stack([zl * 4 + y, dev * labels]).astype(jnp.int32)

    vmem = pl.BlockSpec(memory_space=pltpu.VMEM)
    g, mine, theirs = pl.pallas_call(
        grad_kernel,
        out_shape=(
            jax.ShapeDtypeStruct((rows, labels), BF),
            jax.ShapeDtypeStruct((64, per, 128), F32),
            jax.ShapeDtypeStruct((64, per, 128), BF),
        ),
        in_specs=[pl.BlockSpec(memory_space=pltpu.SMEM), vmem, vmem, pl.BlockSpec(memory_space=pl.ANY), vmem],
        out_specs=(vmem, vmem, vmem),
        scratch_shapes=[
            pltpu.VMEM((rows, width), BF),
            pltpu.VMEM((labels, width), BF),
            pltpu.VMEM((rows, 128), F32),
            pltpu.VMEM((rows, 128), F32),
            pltpu.VMEM((rows, width), F32),
            pltpu.SemaphoreType.DMA((labels // TILE,)),
        ],
        compiler_params=pltpu.CompilerParams(vmem_limit_bytes=40 * 1024 * 1024),
        cost_estimate=pl.CostEstimate(
            flops=4 * rows * labels * width, bytes_accessed=2 * labels * width, transcendentals=2 * rows * labels),
        name="label_grad",
    )(where, own, other, weights, label_bias.reshape(1, labels))

    weight_grad, bias_grad = pl.pallas_call(
        weight_kernel,
        grid=(labels // TILE,),
        out_shape=(
            jax.ShapeDtypeStruct((labels, width), BF),
            jax.ShapeDtypeStruct((1, labels), F32),
        ),
        in_specs=[
            pl.BlockSpec((rows, TILE), lambda t: (0, t)),
            pl.BlockSpec((half, 640), lambda t: (0, 0)),
            pl.BlockSpec((half, 640), lambda t: (0, 0)),
        ],
        out_specs=(pl.BlockSpec((TILE, width), lambda t: (t, 0)), pl.BlockSpec((1, TILE), lambda t: (0, t))),
        cost_estimate=pl.CostEstimate(
            flops=2 * rows * labels * width, bytes_accessed=2 * labels * (width + rows), transcendentals=0),
        name="weight_grad",
    )(g, own, other)

    summed = (mine + xor_permute(theirs, "c", 2, 1).astype(F32)).astype(BF)
    parts = lax.all_to_all(summed, ("x", "zl", "y"), 0, 0)
    total = jnp.sum(parts.astype(F32), axis=0)
    keep = jnp.where(zh == 0, total[:, :64], total[:, 64:])
    send = jnp.where(zh == 0, total[:, 64:], total[:, :64])
    feature_grad = keep + xor_permute(send, "zh", 2, 1)
    return weight_grad, bias_grad.reshape(labels), feature_grad.astype(BF)


def solution(mesh):
    fine = Mesh(mesh.devices.reshape(2, 4, 4, 4, 2), ("zh", "x", "zl", "y", "c"))
    row, col = ("zh", "x"), ("zl", "y", "c")
    return jax.shard_map(
        local,
        mesh=fine,
        in_specs=(P(col, None), P(row + col, None), P(row + col), P(col, None), P(col)),
        out_specs=(P(row + col, None), P(row + col), P(col, row)),
        check_vma=False,
    )
```

```python
import functools

import jax
import jax.numpy as jnp
from jax import lax
from jax.experimental import pallas as pl
from jax.experimental.pallas import tpu as pltpu
from jax.sharding import Mesh, PartitionSpec as P

BF = jnp.bfloat16
F32 = jnp.float32
KEY = 8192
BITS = (0, 3, 2, 1)
CHUNK = 1024
DX_CHUNK = 2048
ROWS_AT_ONCE = 64
SPLIT = 3072
WEIGHT_VMEM = 59 * 1024 * 1024
MIB = 1024 * 1024


def cuts(total, size):
    return [(a, min(size, total - a)) for a in range(0, total, size)]


def xor_permute(x, axis, size, bit):
    return lax.ppermute(x, axis, [(i, i ^ bit) for i in range(size)])


def pack_kernel(*refs):
    *parts, out_ref = refs
    n = parts[0].shape[0]
    for i, part in enumerate(parts):
        out_ref[i * n:(i + 1) * n] = part[...]


def stage_kernel(w_hbm, w_ref, sem):
    copy = pltpu.make_async_copy(w_hbm, w_ref, sem)
    copy.start()
    copy.wait()


def grad_kernel(own_ref, other_ref, w_scr, bias_ref, g_hbm, bg_ref, mine_ref, theirs_ref,
                g_scr, f_scr, first_scr, key_scr, dx_scr, even_scr, odd_scr, sems):
    labels, width = w_scr.shape
    zh, x, zl, y, c = (lax.axis_index(a) for a in ("zh", "x", "zl", "y", "c"))
    dev = (((zh * 4 + x) * 4 + zl) * 4 + y) * 2 + c
    half = own_ref.shape[0]
    rows = 2 * half
    chunks = cuts(labels, CHUNK)
    f_scr[0:half] = own_ref[:, 0:width]
    f_scr[half:rows] = other_ref[:, 0:width]
    f_copy = pltpu.make_async_copy(f_scr, g_hbm.at[:, pl.ds(labels, width)], sems.at[len(chunks)])
    f_copy.start()

    digit = lax.broadcasted_iota(jnp.int32, (128, 128), 0)
    lane = lax.broadcasted_iota(jnp.int32, (128, 128), 1)
    same = (digit % 32) == (lane % 32)
    power = jnp.where(digit < 32, 1.0, jnp.where(digit < 64, 256.0, jnp.where(digit < 96, 65536.0, 0.0)))
    decode = jnp.where(same, power, 0.0).astype(BF)
    offset = (dev * labels).astype(F32)
    row = lax.broadcasted_iota(jnp.int32, (half, 128), 0).astype(F32)
    for h, ref in enumerate((own_ref, other_ref)):
        at = pl.ds(h * half, half)
        local = jnp.dot(ref[:, width:width + 128], decode, preferred_element_type=F32) - offset
        local = jnp.where((local >= 0.0) & (local < float(labels)), local, -1.0)
        first = jnp.max(local, axis=1, keepdims=True)
        first_scr[at] = jnp.broadcast_to(first, (half, 128))
        more = (local >= 0.0) & (local < first)
        key_scr[at] = jnp.where(more, (row + float(h * half)) * float(KEY) + local, -1.0)

    buffers = (even_scr, odd_scr)
    lanes = lax.broadcasted_iota(jnp.int32, (ROWS_AT_ONCE, 128), 1).astype(F32)

    def logits(i):
        a, n = chunks[i]
        buffers[i % 2][:, 0:n] = lax.dot_general(
            f_scr[...], w_scr[a:a + n], (((1,), (1,)), ((), ())), preferred_element_type=F32)

    logits(0)
    for i, (a, n) in enumerate(chunks):
        if i + 1 < len(chunks):
            logits(i + 1)
        for k in range(0, n, 128):
            bias = bias_ref[a + k:a + k + 128].reshape(1, 128)
            for r in range(0, rows, ROWS_AT_ONCE):
                x = buffers[i % 2][r:r + ROWS_AT_ONCE, k:k + 128] + bias
                s = pltpu.reciprocal(1.0 + jnp.exp(-x), approx=True)
                hit = (first_scr[r:r + ROWS_AT_ONCE] - float(a + k)) == lanes
                g_scr[r:r + ROWS_AT_ONCE, a + k:a + k + 128] = jnp.where(hit, s - 1.0, s).astype(BF)

    def one_hit(top):
        key = top.astype(jnp.int32)
        b = key // KEY
        l = key - b * KEY
        b16 = pl.ds(pl.multiple_of((b // 16) * 16, 16), 16)
        l128 = pl.ds(pl.multiple_of((l // 128) * 128, 128), 128)
        r = lax.broadcasted_iota(jnp.int32, (16, 128), 0)
        c = lax.broadcasted_iota(jnp.int32, (16, 128), 1)
        old = g_scr[b16, l128].astype(F32)
        g_scr[b16, l128] = jnp.where((r == b % 16) & (c == l % 128), old - 1.0, old).astype(BF)
        keys = key_scr[...]
        keys = jnp.where(keys == top, -1.0, keys)
        key_scr[...] = keys
        return jnp.max(keys)

    lax.while_loop(lambda top: top >= 0.0, one_hit, jnp.max(key_scr[...]))
    g_copies = [
        pltpu.make_async_copy(g_scr.at[:, pl.ds(a, n)], g_hbm.at[:, pl.ds(a, n)], sems.at[i])
        for i, (a, n) in enumerate(chunks)
    ]
    for copy in g_copies:
        copy.start()
    for a, n in chunks:
        bg_ref[a:a + n] = jnp.sum(g_scr[:, a:a + n].astype(F32), axis=0)

    for j, (a, n) in enumerate(cuts(labels, DX_CHUNK)):
        term = jnp.dot(g_scr[:, a:a + n], w_scr[a:a + n], preferred_element_type=F32)
        if j == 0:
            dx_scr[0:rows] = term
        else:
            dx_scr[0:rows] += term
    dx_scr[rows:rows + 16] = jnp.zeros((16, width), F32)

    low = lax.broadcasted_iota(jnp.int32, (half + 16, 128), 1) < 64
    per, block = half // 16, mine_ref.shape[2]
    for jc, ref in enumerate((mine_ref, theirs_ref)):
        at = pl.ds(jc * half, half + 16)
        for to_x in range(4):
            k = (to_x // 2) * 128
            left = dx_scr[at, k:k + 128]
            right = dx_scr[at, 256 + k:256 + k + 128]
            if to_x % 2 == 0:
                both = jnp.where(low, left, pltpu.roll(right, 64, 1))
            else:
                both = jnp.where(low, pltpu.roll(left, 64, 1), right)
            for pz, jz in enumerate(BITS):
                for py, jy in enumerate(BITS):
                    j = (pz * 4 + py) * per
                    ref[to_x * 4 + (y ^ jy), zl ^ jz] = both[j:j + block].astype(ref.dtype)
    for copy in g_copies:
        copy.wait()
    f_copy.wait()


def weight_kernel(begin, end, g_hbm, *refs):
    wg_hbm, g_scr, f_scr, out_scr, g_sems, out_sems, f_sem = refs[-7:]
    chunks = cuts(end - begin, CHUNK)
    labels, width = wg_hbm.shape
    f_copy = pltpu.make_async_copy(g_hbm.at[:, pl.ds(labels, width)], f_scr, f_sem)
    f_copy.start()
    g_copies = [
        pltpu.make_async_copy(g_hbm.at[:, pl.ds(begin + a, n)], g_scr.at[:, pl.ds(a, n)], g_sems.at[i])
        for i, (a, n) in enumerate(chunks)
    ]
    out_copies = [
        pltpu.make_async_copy(out_scr.at[pl.ds(a, n)], wg_hbm.at[pl.ds(begin + a, n)], out_sems.at[i])
        for i, (a, n) in enumerate(chunks)
    ]
    for copy in g_copies:
        copy.start()
    f_copy.wait()
    for i, (a, n) in enumerate(chunks):
        g_copies[i].wait()
        g = g_scr[:, a:a + n]
        out_scr[a:a + n] = lax.dot_general(
            g, f_scr[...], (((0,), (0,)), ((), ())), preferred_element_type=F32).astype(BF)
        out_copies[i].start()
    for copy in out_copies:
        copy.wait()


def local(features, weights, label_bias, pos_ids, pos_count):
    labels, width = weights.shape
    per, slots = pos_ids.shape
    half = per * 16
    rows = 2 * half
    wide = width + 4 * slots
    vmem = pl.BlockSpec(memory_space=pltpu.VMEM)
    hbm = pl.BlockSpec(memory_space=pltpu.HBM)
    n_chunks = len(cuts(labels, CHUNK))

    slot = jnp.arange(slots, dtype=jnp.int32)
    ids = jnp.where(slot[None, :] < pos_count[:, None], pos_ids, 0xFFFFFF)
    pay = jnp.pad(features, ((0, 0), (0, wide - width)))
    for k in range(3):
        at = width + k * slots
        pay = pay + jnp.pad(((ids >> (8 * k)) & 255).astype(BF), ((0, 0), (at, wide - at - slots)))
    pay = jnp.concatenate([pay] + [xor_permute(pay, "y", 4, d) for d in BITS[1:]], axis=0)
    pay, weights_then = lax.optimization_barrier((pay, weights))
    staged = pl.pallas_call(
        stage_kernel,
        out_shape=jax.ShapeDtypeStruct((labels, width), BF),
        in_specs=[hbm],
        out_specs=vmem,
        scratch_shapes=[pltpu.SemaphoreType.DMA],
        compiler_params=pltpu.CompilerParams(vmem_limit_bytes=46 * MIB),
        cost_estimate=pl.CostEstimate(flops=0, bytes_accessed=4 * labels * width, transcendentals=0),
        name="stage_weights",
    )(weights_then)
    zs = [xor_permute(pay, "zl", 4, d) for d in BITS[1:]]
    staged, *zs = lax.optimization_barrier((staged, *zs))
    own = pl.pallas_call(
        pack_kernel,
        out_shape=jax.ShapeDtypeStruct((half, wide), BF),
        in_specs=[vmem] * 4,
        out_specs=vmem,
        compiler_params=pltpu.CompilerParams(vmem_limit_bytes=4 * MIB),
        name="pack",
    )(pay, *zs)
    other = xor_permute(own, "c", 2, 1)

    g, bias_grad, mine, theirs = pl.pallas_call(
        grad_kernel,
        out_shape=(
            jax.ShapeDtypeStruct((rows, 2 * labels), BF),
            jax.ShapeDtypeStruct((labels,), F32),
            jax.ShapeDtypeStruct((16, 4, 16, 128), F32),
            jax.ShapeDtypeStruct((16, 4, 16, 128), BF),
        ),
        in_specs=[vmem] * 4,
        out_specs=(hbm, vmem, vmem, vmem),
        scratch_shapes=[
            pltpu.VMEM((rows, labels), BF),
            pltpu.VMEM((rows, width), BF),
            pltpu.VMEM((rows, 128), F32),
            pltpu.VMEM((rows, 128), F32),
            pltpu.VMEM((rows + 16, width), F32),
            pltpu.VMEM((rows, CHUNK), F32),
            pltpu.VMEM((rows, CHUNK), F32),
            pltpu.SemaphoreType.DMA((n_chunks + 1,)),
        ],
        compiler_params=pltpu.CompilerParams(vmem_limit_bytes=44 * MIB),
        cost_estimate=pl.CostEstimate(
            flops=4 * rows * labels * width, bytes_accessed=2 * labels * (width + rows),
            transcendentals=2 * rows * labels),
        name="label_grad",
    )(own, other, staged, label_bias)

    send = (mine + xor_permute(theirs, "c", 2, 1).astype(F32)).astype(BF)
    parts = lax.all_to_all(send, ("x", "y"), 0, 0)

    def weight_part(begin, end, *before):
        n = len(cuts(end - begin, CHUNK))
        return pl.pallas_call(
            functools.partial(weight_kernel, begin, end),
            out_shape=jax.ShapeDtypeStruct((labels, width), BF),
            in_specs=[hbm] * (1 + len(before)),
            out_specs=hbm,
            input_output_aliases={1: 0} if before else {},
            scratch_shapes=[
                pltpu.VMEM((rows, end - begin), BF),
                pltpu.VMEM((rows, width), BF),
                pltpu.VMEM((end - begin, width), BF),
                pltpu.SemaphoreType.DMA((n,)),
                pltpu.SemaphoreType.DMA((n,)),
                pltpu.SemaphoreType.DMA,
            ],
            compiler_params=pltpu.CompilerParams(vmem_limit_bytes=WEIGHT_VMEM),
            cost_estimate=pl.CostEstimate(
                flops=2 * rows * (end - begin) * width, bytes_accessed=2 * (end - begin) * (width + rows),
                transcendentals=0),
            name="weight_grad",
        )(g, *before)

    weight_grad = weight_part(0, SPLIT)
    total = jnp.sum(parts.astype(F32), axis=0)
    total, weight_grad = lax.optimization_barrier((total, weight_grad))
    weight_grad = weight_part(SPLIT, labels, weight_grad)
    blocks = lax.all_to_all(jnp.concatenate([total, total]), ("zh", "zl"), 0, 0)
    total = jnp.sum(blocks, axis=0)[:per]
    feature_grad = jnp.where(lax.axis_index("zh") == 0, total[:, :64], total[:, 64:]).astype(BF)
    return weight_grad, bias_grad, feature_grad


def solution(mesh):
    fine = Mesh(mesh.devices.reshape(2, 4, 4, 4, 2), ("zh", "x", "zl", "y", "c"))
    row, col = ("zh", "x"), ("zl", "y", "c")
    return jax.shard_map(
        local,
        mesh=fine,
        in_specs=(P(col, None), P(row + col, None), P(row + col), P(col, None), P(col)),
        out_specs=(P(row + col, None), P(row + col), P(col, row)),
        check_vma=False,
    )
```

```python
import functools

import jax
import jax.numpy as jnp
from jax import lax
from jax.experimental import pallas as pl
from jax.experimental.pallas import tpu as pltpu
from jax.sharding import Mesh, PartitionSpec as P

BF = jnp.bfloat16
F32 = jnp.float32
KEY = 8192
BITS = (0, 3, 2, 1)
CHUNK = 1024
DX_CHUNK = 2048
ROWS_AT_ONCE = 64
SPLIT = 3072
MIB = 1024 * 1024
WEIGHT_VMEM = 50 * MIB
OTHER_VMEM = 43 * MIB


def cuts(total, size):
    return [(a, min(size, total - a)) for a in range(0, total, size)]


def xor_permute(x, axis, size, bit):
    return lax.ppermute(x, axis, [(i, i ^ bit) for i in range(size)])


def pack_kernel(*refs):
    *parts, out_ref = refs
    n = parts[0].shape[0]
    for i, part in enumerate(parts):
        out_ref[i * n:(i + 1) * n] = part[...]


def stage_kernel(w_hbm, w_ref, sem):
    copy = pltpu.make_async_copy(w_hbm, w_ref, sem)
    copy.start()
    copy.wait()


def half_grad(first_row, rows_ref, w_ref, bias_ref, g_ref, first_scr, key_scr, even_scr, odd_scr):
    labels, width = w_ref.shape
    half = rows_ref.shape[0]
    chunks = cuts(labels, CHUNK)
    zh, x, zl, y, c = (lax.axis_index(a) for a in ("zh", "x", "zl", "y", "c"))
    offset = ((((zh * 4 + x) * 4 + zl) * 4 + y) * 2 + c) * labels

    digit = lax.broadcasted_iota(jnp.int32, (128, 128), 0)
    lane = lax.broadcasted_iota(jnp.int32, (128, 128), 1)
    same = (digit % 32) == (lane % 32)
    power = jnp.where(digit < 32, 1.0, jnp.where(digit < 64, 256.0, jnp.where(digit < 96, 65536.0, 0.0)))
    decode = jnp.where(same, power, 0.0).astype(BF)
    row = lax.broadcasted_iota(jnp.int32, (half, 128), 0).astype(F32)
    local = jnp.dot(rows_ref[:, width:width + 128], decode, preferred_element_type=F32) - offset.astype(F32)
    local = jnp.where((local >= 0.0) & (local < float(labels)), local, -1.0)
    first = jnp.max(local, axis=1, keepdims=True)
    first_scr[...] = jnp.broadcast_to(first, (half, 128))
    more = (local >= 0.0) & (local < first)
    key_scr[...] = jnp.where(more, row * float(KEY) + local, -1.0)

    buffers = (even_scr, odd_scr)
    lanes = lax.broadcasted_iota(jnp.int32, (ROWS_AT_ONCE, 128), 1).astype(F32)

    def logits(i):
        a, n = chunks[i]
        buffers[i % 2][:, 0:n] = lax.dot_general(
            rows_ref[:, 0:width], w_ref[a:a + n], (((1,), (1,)), ((), ())), preferred_element_type=F32)

    logits(0)
    for i, (a, n) in enumerate(chunks):
        if i + 1 < len(chunks):
            logits(i + 1)
        for k in range(0, n, 128):
            bias = bias_ref[a + k:a + k + 128].reshape(1, 128)
            for r in range(0, half, ROWS_AT_ONCE):
                x = buffers[i % 2][r:r + ROWS_AT_ONCE, k:k + 128] + bias
                s = pltpu.reciprocal(1.0 + jnp.exp(-x), approx=True)
                hit = (first_scr[r:r + ROWS_AT_ONCE] - float(a + k)) == lanes
                g_ref[r:r + ROWS_AT_ONCE, a + k:a + k + 128] = jnp.where(hit, s - 1.0, s).astype(BF)

    def one_hit(top):
        key = top.astype(jnp.int32)
        b = key // KEY
        l = key - b * KEY
        b16 = pl.ds(pl.multiple_of((b // 16) * 16, 16), 16)
        l128 = pl.ds(pl.multiple_of((l // 128) * 128, 128), 128)
        r = lax.broadcasted_iota(jnp.int32, (16, 128), 0)
        c = lax.broadcasted_iota(jnp.int32, (16, 128), 1)
        old = g_ref[b16, l128].astype(F32)
        g_ref[b16, l128] = jnp.where((r == b % 16) & (c == l % 128), old - 1.0, old).astype(BF)
        keys = key_scr[...]
        keys = jnp.where(keys == top, -1.0, keys)
        key_scr[...] = keys
        return jnp.max(keys)

    lax.while_loop(lambda top: top >= 0.0, one_hit, jnp.max(key_scr[...]))


def half_dx(g_ref, w_ref, dx_scr, out_ref):
    labels, width = w_ref.shape
    half = g_ref.shape[0]
    for j, (a, n) in enumerate(cuts(labels, DX_CHUNK)):
        term = jnp.dot(g_ref[:, a:a + n], w_ref[a:a + n], preferred_element_type=F32)
        if j == 0:
            dx_scr[0:half] = term
        else:
            dx_scr[0:half] += term
    dx_scr[half:half + 16] = jnp.zeros((16, width), F32)
    zl, y = lax.axis_index("zl"), lax.axis_index("y")
    low = lax.broadcasted_iota(jnp.int32, (half + 16, 128), 1) < 64
    per, block = half // 16, out_ref.shape[2]
    for to_x in range(4):
        k = (to_x // 2) * 128
        left = dx_scr[:, k:k + 128]
        right = dx_scr[:, 256 + k:256 + k + 128]
        if to_x % 2 == 0:
            both = jnp.where(low, left, pltpu.roll(right, 64, 1))
        else:
            both = jnp.where(low, pltpu.roll(left, 64, 1), right)
        for pz, jz in enumerate(BITS):
            for py, jy in enumerate(BITS):
                j = (pz * 4 + py) * per
                out_ref[to_x * 4 + (y ^ jy), zl ^ jz] = both[j:j + block].astype(out_ref.dtype)


def own_kernel(own_ref, w_ref, bias_ref, g_ref, *scratch):
    half_grad(0, own_ref, w_ref, bias_ref, g_ref, *scratch)


def other_kernel(own_ref, other_ref, g_own_ref, w_ref, bias_ref, g_hbm, theirs_ref,
                 g_scr, dx_scr, first_scr, key_scr, even_scr, odd_scr, sems):
    labels, width = w_ref.shape
    half = own_ref.shape[0]
    low, high = pl.ds(0, half), pl.ds(half, half)
    body, tail = pl.ds(0, labels), pl.ds(labels, width)
    early = [
        pltpu.make_async_copy(g_own_ref, g_hbm.at[low, body], sems.at[0]),
        pltpu.make_async_copy(own_ref.at[:, pl.ds(0, width)], g_hbm.at[low, tail], sems.at[1]),
        pltpu.make_async_copy(other_ref.at[:, pl.ds(0, width)], g_hbm.at[high, tail], sems.at[2]),
    ]
    for copy in early:
        copy.start()
    half_grad(half, other_ref, w_ref, bias_ref, g_scr, first_scr, key_scr, even_scr, odd_scr)
    late = pltpu.make_async_copy(g_scr, g_hbm.at[high, body], sems.at[3])
    late.start()
    half_dx(g_scr, w_ref, dx_scr, theirs_ref)
    for copy in early + [late]:
        copy.wait()


def own_dx_kernel(g_ref, w_ref, mine_ref, dx_scr):
    half_dx(g_ref, w_ref, dx_scr, mine_ref)


def join_kernel(mine_ref, received_ref, out_ref):
    out_ref[...] = (mine_ref[...] + received_ref[...].astype(F32)).astype(BF)


def plane_sum_kernel(parts_ref, out_ref):
    total = jnp.sum(parts_ref[...].astype(F32), axis=0)
    out_ref[0:4] = total
    out_ref[4:8] = total


def weight_kernel(begin, end, g_hbm, *refs):
    wg_hbm, bg_hbm, g_scr, f_scr, out_scr, bias_scr, g_sems, out_sems, f_sem, bias_sem = refs[-10:]
    chunks = cuts(end - begin, CHUNK)
    labels, width = wg_hbm.shape
    f_copy = pltpu.make_async_copy(g_hbm.at[:, pl.ds(labels, width)], f_scr, f_sem)
    f_copy.start()
    g_copies = [
        pltpu.make_async_copy(g_hbm.at[:, pl.ds(begin + a, n)], g_scr.at[:, pl.ds(a, n)], g_sems.at[i])
        for i, (a, n) in enumerate(chunks)
    ]
    out_copies = [
        pltpu.make_async_copy(out_scr.at[pl.ds(a, n)], wg_hbm.at[pl.ds(begin + a, n)], out_sems.at[i])
        for i, (a, n) in enumerate(chunks)
    ]
    for copy in g_copies:
        copy.start()
    f_copy.wait()
    for i, (a, n) in enumerate(chunks):
        g_copies[i].wait()
        g = g_scr[:, a:a + n]
        out_scr[a:a + n] = lax.dot_general(
            g, f_scr[...], (((0,), (0,)), ((), ())), preferred_element_type=F32).astype(BF)
        out_copies[i].start()
        bias_scr[a:a + n] = jnp.sum(g.astype(F32), axis=0)
    bias_copy = pltpu.make_async_copy(bias_scr, bg_hbm.at[pl.ds(begin, end - begin)], bias_sem)
    bias_copy.start()
    for copy in out_copies + [bias_copy]:
        copy.wait()


def local(features, weights, label_bias, pos_ids, pos_count):
    labels, width = weights.shape
    per, slots = pos_ids.shape
    half = per * 16
    rows = 2 * half
    wide = width + 4 * slots
    vmem = pl.BlockSpec(memory_space=pltpu.VMEM)
    hbm = pl.BlockSpec(memory_space=pltpu.HBM)
    n_chunks = len(cuts(labels, CHUNK))

    slot = jnp.arange(slots, dtype=jnp.int32)
    ids = jnp.where(slot[None, :] < pos_count[:, None], pos_ids, 0xFFFFFF)
    pay = jnp.pad(features, ((0, 0), (0, wide - width)))
    for k in range(3):
        at = width + k * slots
        pay = pay + jnp.pad(((ids >> (8 * k)) & 255).astype(BF), ((0, 0), (at, wide - at - slots)))
    pay = jnp.concatenate([pay] + [xor_permute(pay, "y", 4, d) for d in BITS[1:]], axis=0)
    pay, weights_then = lax.optimization_barrier((pay, weights))
    staged = pl.pallas_call(
        stage_kernel,
        out_shape=jax.ShapeDtypeStruct((labels, width), BF),
        in_specs=[hbm],
        out_specs=vmem,
        scratch_shapes=[pltpu.SemaphoreType.DMA],
        compiler_params=pltpu.CompilerParams(vmem_limit_bytes=46 * MIB),
        cost_estimate=pl.CostEstimate(flops=0, bytes_accessed=4 * labels * width, transcendentals=0),
        name="stage_weights",
    )(weights_then)
    zs = [xor_permute(pay, "zl", 4, d) for d in BITS[1:]]
    staged, *zs = lax.optimization_barrier((staged, *zs))
    own = pl.pallas_call(
        pack_kernel,
        out_shape=jax.ShapeDtypeStruct((half, wide), BF),
        in_specs=[vmem] * 4,
        out_specs=vmem,
        compiler_params=pltpu.CompilerParams(vmem_limit_bytes=4 * MIB),
        name="pack",
    )(pay, *zs)
    other = xor_permute(own, "c", 2, 1)

    half_scratch = [
        pltpu.VMEM((half, 128), F32),
        pltpu.VMEM((half, 128), F32),
        pltpu.VMEM((half, CHUNK), F32),
        pltpu.VMEM((half, CHUNK), F32),
    ]
    dx_scratch = pltpu.VMEM((half + 16, width), F32)
    blocks_of = functools.partial(jax.ShapeDtypeStruct, (16, 4, 16, 128))
    product = 2 * half * labels * width
    g_own = pl.pallas_call(
        own_kernel,
        out_shape=jax.ShapeDtypeStruct((half, labels), BF),
        in_specs=[vmem] * 3,
        out_specs=vmem,
        scratch_shapes=half_scratch,
        compiler_params=pltpu.CompilerParams(vmem_limit_bytes=16 * MIB),
        cost_estimate=pl.CostEstimate(
            flops=product, bytes_accessed=2 * labels * width, transcendentals=2 * half * labels),
        name="own_label_grad",
    )(own, staged, label_bias)
    g, theirs = pl.pallas_call(
        other_kernel,
        out_shape=(
            jax.ShapeDtypeStruct((rows, 3 * labels), BF),
            blocks_of(BF),
        ),
        in_specs=[vmem] * 5,
        out_specs=(hbm, vmem),
        scratch_shapes=[pltpu.VMEM((half, labels), BF), dx_scratch] + half_scratch + [pltpu.SemaphoreType.DMA((4,))],
        compiler_params=pltpu.CompilerParams(vmem_limit_bytes=OTHER_VMEM),
        cost_estimate=pl.CostEstimate(
            flops=2 * product, bytes_accessed=2 * labels * width, transcendentals=2 * half * labels),
        name="other_label_grad",
    )(own, other, g_own, staged, label_bias)
    received = xor_permute(theirs, "c", 2, 1)
    mine = pl.pallas_call(
        own_dx_kernel,
        out_shape=blocks_of(F32),
        in_specs=[vmem] * 2,
        out_specs=vmem,
        scratch_shapes=[dx_scratch],
        compiler_params=pltpu.CompilerParams(vmem_limit_bytes=16 * MIB),
        cost_estimate=pl.CostEstimate(flops=product, bytes_accessed=2 * labels * width, transcendentals=0),
        name="own_dx",
    )(g_own, staged)
    send = pl.pallas_call(
        join_kernel,
        out_shape=blocks_of(BF),
        in_specs=[vmem] * 2,
        out_specs=vmem,
        compiler_params=pltpu.CompilerParams(vmem_limit_bytes=16 * MIB),
        name="join",
    )(mine, received)
    send, g = lax.optimization_barrier((send, g))
    parts = lax.all_to_all(send, ("x", "y"), 0, 0)

    def weight_part(begin, end, *before):
        n = len(cuts(end - begin, CHUNK))
        return pl.pallas_call(
            functools.partial(weight_kernel, begin, end),
            out_shape=(jax.ShapeDtypeStruct((labels, width), BF), jax.ShapeDtypeStruct((labels,), F32)),
            in_specs=[hbm] * (1 + len(before)),
            out_specs=(hbm, hbm),
            input_output_aliases={1: 0, 2: 1} if before else {},
            scratch_shapes=[
                pltpu.VMEM((rows, end - begin), BF),
                pltpu.VMEM((rows, width), BF),
                pltpu.VMEM((end - begin, width), BF),
                pltpu.VMEM((end - begin,), F32),
                pltpu.SemaphoreType.DMA((n,)),
                pltpu.SemaphoreType.DMA((n,)),
                pltpu.SemaphoreType.DMA,
                pltpu.SemaphoreType.DMA,
            ],
            compiler_params=pltpu.CompilerParams(vmem_limit_bytes=WEIGHT_VMEM),
            cost_estimate=pl.CostEstimate(
                flops=2 * rows * (end - begin) * width, bytes_accessed=2 * (end - begin) * (width + rows),
                transcendentals=0),
            name="weight_grad",
        )(g, *before)

    weight_grad, bias_grad = weight_part(0, SPLIT)
    blocks = pl.pallas_call(
        plane_sum_kernel,
        out_shape=jax.ShapeDtypeStruct((8, 16, 128), F32),
        in_specs=[vmem],
        out_specs=vmem,
        compiler_params=pltpu.CompilerParams(vmem_limit_bytes=16 * MIB),
        name="plane_sum",
    )(parts)
    blocks, weight_grad, bias_grad = lax.optimization_barrier((blocks, weight_grad, bias_grad))
    weight_grad, bias_grad = weight_part(SPLIT, labels, weight_grad, bias_grad)
    blocks = lax.all_to_all(blocks, ("zh", "zl"), 0, 0)
    total = jnp.sum(blocks, axis=0)[:per]
    feature_grad = jnp.where(lax.axis_index("zh") == 0, total[:, :64], total[:, 64:]).astype(BF)
    return weight_grad, bias_grad, feature_grad


def solution(mesh):
    fine = Mesh(mesh.devices.reshape(2, 4, 4, 4, 2), ("zh", "x", "zl", "y", "c"))
    row, col = ("zh", "x"), ("zl", "y", "c")
    return jax.shard_map(
        local,
        mesh=fine,
        in_specs=(P(col, None), P(row + col, None), P(row + col), P(col, None), P(col)),
        out_specs=(P(row + col, None), P(row + col), P(col, row)),
        check_vma=False,
    )
```

```python
import functools

import jax
import jax.numpy as jnp
import numpy as np
from jax import lax
from jax.experimental import pallas as pl
from jax.experimental.pallas import tpu as pltpu
from jax.sharding import Mesh, PartitionSpec as P

BF = jnp.bfloat16
F32 = jnp.float32
KEY = 8192
BITS = (0, 3, 2, 1)
CHUNK = 1024
DX_CHUNK = 2048
ROWS_AT_ONCE = 64
MIB = 1024 * 1024
WEIGHT_VMEM = 50 * MIB
OTHER_VMEM = 38 * MIB


def cuts(total, size):
    return [(a, min(size, total - a)) for a in range(0, total, size)]


def xor_permute(x, axis, size, bit):
    return lax.ppermute(x, axis, [(i, i ^ bit) for i in range(size)])


def pack_kernel(*refs):
    *parts, out_ref = refs
    n = parts[0].shape[0]
    for i, part in enumerate(parts):
        out_ref[i * n:(i + 1) * n] = part[...]


def stage_kernel(w_hbm, w_ref, sem):
    copy = pltpu.make_async_copy(w_hbm, w_ref, sem)
    copy.start()
    copy.wait()


def half_grad(rows_ref, w_ref, bias_ref, g_ref, first_scr, key_scr, even_scr, odd_scr):
    labels, width = w_ref.shape
    half = rows_ref.shape[0]
    chunks = cuts(labels, CHUNK)
    zh, x, zl, y, c = (lax.axis_index(a) for a in ("zh", "x", "zl", "y", "c"))
    offset = ((((zh * 4 + x) * 4 + zl) * 4 + y) * 2 + c) * labels

    digit = lax.broadcasted_iota(jnp.int32, (128, 128), 0)
    lane = lax.broadcasted_iota(jnp.int32, (128, 128), 1)
    same = (digit % 32) == (lane % 32)
    power = jnp.where(digit < 32, 1.0, jnp.where(digit < 64, 256.0, jnp.where(digit < 96, 65536.0, 0.0)))
    decode = jnp.where(same, power, 0.0).astype(BF)
    row = lax.broadcasted_iota(jnp.int32, (half, 128), 0).astype(F32)
    local = jnp.dot(rows_ref[:, width:width + 128], decode, preferred_element_type=F32) - offset.astype(F32)
    local = jnp.where((local >= 0.0) & (local < float(labels)), local, -1.0)
    first = jnp.max(local, axis=1, keepdims=True)
    first_scr[...] = jnp.broadcast_to(first, (half, 128))
    more = (local >= 0.0) & (local < first)
    key_scr[...] = jnp.where(more, row * float(KEY) + local, -1.0)

    buffers = (even_scr, odd_scr)
    lanes = lax.broadcasted_iota(jnp.int32, (ROWS_AT_ONCE, 128), 1).astype(F32)

    def logits(i):
        a, n = chunks[i]
        buffers[i % 2][:, 0:n] = lax.dot_general(
            rows_ref[:, 0:width], w_ref[a:a + n], (((1,), (1,)), ((), ())), preferred_element_type=F32)

    logits(0)
    for i, (a, n) in enumerate(chunks):
        if i + 1 < len(chunks):
            logits(i + 1)
        for k in range(0, n, 128):
            bias = bias_ref[a + k:a + k + 128].reshape(1, 128)
            for r in range(0, half, ROWS_AT_ONCE):
                x = buffers[i % 2][r:r + ROWS_AT_ONCE, k:k + 128] + bias
                s = pltpu.reciprocal(1.0 + jnp.exp(-x), approx=True)
                hit = (first_scr[r:r + ROWS_AT_ONCE] - float(a + k)) == lanes
                g_ref[r:r + ROWS_AT_ONCE, a + k:a + k + 128] = jnp.where(hit, s - 1.0, s).astype(BF)

    def one_hit(top):
        key = top.astype(jnp.int32)
        b = key // KEY
        l = key - b * KEY
        b16 = pl.ds(pl.multiple_of((b // 16) * 16, 16), 16)
        l128 = pl.ds(pl.multiple_of((l // 128) * 128, 128), 128)
        r = lax.broadcasted_iota(jnp.int32, (16, 128), 0)
        c = lax.broadcasted_iota(jnp.int32, (16, 128), 1)
        old = g_ref[b16, l128].astype(F32)
        g_ref[b16, l128] = jnp.where((r == b % 16) & (c == l % 128), old - 1.0, old).astype(BF)
        keys = key_scr[...]
        keys = jnp.where(keys == top, -1.0, keys)
        key_scr[...] = keys
        return jnp.max(keys)

    lax.while_loop(lambda top: top >= 0.0, one_hit, jnp.max(key_scr[...]))


def half_dx(g_ref, w_ref, dx_scr, out_ref):
    labels, width = w_ref.shape
    half = g_ref.shape[0]
    for j, (a, n) in enumerate(cuts(labels, DX_CHUNK)):
        term = jnp.dot(g_ref[:, a:a + n], w_ref[a:a + n], preferred_element_type=F32)
        if j == 0:
            dx_scr[0:half] = term
        else:
            dx_scr[0:half] += term
    dx_scr[half:half + 16] = jnp.zeros((16, width), F32)
    zl, y = lax.axis_index("zl"), lax.axis_index("y")
    low = lax.broadcasted_iota(jnp.int32, (8, 128), 1) < 64
    per = half // 16
    for k in range(width // 128):
        here = dx_scr[:, k * 128:(k + 1) * 128]
        turned = pltpu.roll(here, 64, 1)
        for pz, jz in enumerate(BITS):
            for py, jy in enumerate(BITS):
                j = (pz * 4 + py) * per
                to_chip = (zl ^ jz) * 4 + (y ^ jy)
                m = j + per // 2
                even = jnp.where(low, here[j:j + 8], turned[m:m + 8])
                odd = jnp.where(low, turned[j:j + 8], here[m:m + 8])
                out_ref[32 * k + to_chip] = even.astype(out_ref.dtype)
                out_ref[32 * k + 16 + to_chip] = odd.astype(out_ref.dtype)


def own_kernel(own_ref, w_ref, bias_ref, g_ref, *scratch):
    half_grad(own_ref, w_ref, bias_ref, g_ref, *scratch)


def other_kernel(own_ref, other_ref, g_own_ref, w_ref, bias_ref, g_hbm, g_ref, theirs_ref, dx_scr, first_scr, key_scr, even_scr, odd_scr, sems):
    width = w_ref.shape[1]
    cols = pl.ds(0, width)
    early = [
        pltpu.make_async_copy(g_own_ref, g_hbm.at[0], sems.at[0]),
        pltpu.make_async_copy(own_ref.at[:, cols], g_hbm.at[2, :, cols], sems.at[1]),
        pltpu.make_async_copy(other_ref.at[:, cols], g_hbm.at[3, :, cols], sems.at[2]),
    ]
    for copy in early:
        copy.start()
    half_grad(other_ref, w_ref, bias_ref, g_ref, first_scr, key_scr, even_scr, odd_scr)
    half_dx(g_ref, w_ref, dx_scr, theirs_ref)
    for copy in early:
        copy.wait()


def own_dx_kernel(g_ref, w_ref, g_other_ref, _, mine_ref, g_hbm, dx_scr, sem):
    copy = pltpu.make_async_copy(g_other_ref, g_hbm.at[1], sem)
    copy.start()
    half_dx(g_ref, w_ref, dx_scr, mine_ref)
    copy.wait()


def join_kernel(mine_ref, received_ref, out_ref):
    out_ref[...] = (mine_ref[...] + received_ref[...].astype(F32)).astype(BF)


def total_kernel(parts_ref, out_ref):
    total = jnp.sum(parts_ref[...].astype(F32), axis=0)
    per, cols = out_ref.shape
    out_ref[0:per // 2] = total[0:per // 2, 0:cols].astype(BF)
    out_ref[per // 2:per] = total[0:per // 2, cols:2 * cols].astype(BF)


def weight_kernel(g_hbm, wg_hbm, bg_hbm, g_scr, f_scr, out_scr, bias_scr, g_sems, out_sems, f_sems, bias_sem):
    labels, width = wg_hbm.shape
    chunks = cuts(labels, CHUNK)
    half = g_hbm.shape[1]
    halves = [pl.ds(0, half), pl.ds(half, half)]
    f_copies = [
        pltpu.make_async_copy(g_hbm.at[2 + h, :, pl.ds(0, width)], f_scr.at[at], f_sems.at[h])
        for h, at in enumerate(halves)
    ]
    g_copies = [
        pltpu.make_async_copy(g_hbm.at[h, :, pl.ds(a, n)], g_scr.at[at, pl.ds(a, n)], g_sems.at[2 * i + h])
        for i, (a, n) in enumerate(chunks) for h, at in enumerate(halves)
    ]
    out_copies = [
        pltpu.make_async_copy(out_scr.at[pl.ds(a, n)], wg_hbm.at[pl.ds(a, n)], out_sems.at[i])
        for i, (a, n) in enumerate(chunks)
    ]
    for copy in f_copies + g_copies:
        copy.start()
    for copy in f_copies:
        copy.wait()
    for i, (a, n) in enumerate(chunks):
        g_copies[2 * i].wait()
        g_copies[2 * i + 1].wait()
        g = g_scr[:, a:a + n]
        out_scr[a:a + n] = lax.dot_general(
            g, f_scr[...], (((0,), (0,)), ((), ())), preferred_element_type=F32).astype(BF)
        out_copies[i].start()
        bias_scr[a:a + n] = jnp.sum(g.astype(F32), axis=0)
    bias_copy = pltpu.make_async_copy(bias_scr, bg_hbm, bias_sem)
    bias_copy.start()
    for copy in out_copies + [bias_copy]:
        copy.wait()


def local(features, weights, label_bias, pos_ids, pos_count):
    labels, width = weights.shape
    per, slots = pos_ids.shape
    half = per * 16
    rows = 2 * half
    wide = width + 4 * slots
    vmem = pl.BlockSpec(memory_space=pltpu.VMEM)
    hbm = pl.BlockSpec(memory_space=pltpu.HBM)
    n_chunks = len(cuts(labels, CHUNK))

    lane = np.arange(wide) - width
    slot = np.where(lane < 0, 0, lane % slots).astype(np.int32)
    shift = (8 * np.clip(lane // slots, 0, 2)).astype(np.int32)
    ids = sum(
        jnp.pad(pos_ids, ((0, 0), (width + k * slots, (3 - k) * slots))) for k in range(3))
    ids = jnp.where(slot[None, :] < pos_count[:, None], ids, 0xFFFFFF)
    digits = lax.shift_right_logical(ids, jnp.broadcast_to(shift[None, :], ids.shape)) & 255
    pay = jnp.where(
        (lane < 0)[None, :], jnp.pad(features, ((0, 0), (0, wide - width))), digits.astype(BF))
    pay = jnp.concatenate([pay] + [xor_permute(pay, "y", 4, d) for d in BITS[1:]], axis=0)
    pay, weights_then = lax.optimization_barrier((pay, weights))
    staged = pl.pallas_call(
        stage_kernel,
        out_shape=jax.ShapeDtypeStruct((labels, width), BF),
        in_specs=[hbm],
        out_specs=vmem,
        scratch_shapes=[pltpu.SemaphoreType.DMA],
        compiler_params=pltpu.CompilerParams(vmem_limit_bytes=46 * MIB),
        cost_estimate=pl.CostEstimate(flops=0, bytes_accessed=4 * labels * width, transcendentals=0),
        name="stage_weights",
    )(weights_then)
    zs = [xor_permute(pay, "zl", 4, d) for d in BITS[1:]]
    staged, *zs = lax.optimization_barrier((staged, *zs))
    own = pl.pallas_call(
        pack_kernel,
        out_shape=jax.ShapeDtypeStruct((half, wide), BF),
        in_specs=[vmem] * 4,
        out_specs=vmem,
        compiler_params=pltpu.CompilerParams(vmem_limit_bytes=4 * MIB),
        name="pack",
    )(pay, *zs)
    other = xor_permute(own, "c", 2, 1)

    half_scratch = [
        pltpu.VMEM((half, 128), F32),
        pltpu.VMEM((half, 128), F32),
        pltpu.VMEM((half, CHUNK), F32),
        pltpu.VMEM((half, CHUNK), F32),
    ]
    dx_scratch = pltpu.VMEM((half + 16, width), F32)
    blocks_of = functools.partial(jax.ShapeDtypeStruct, (128, 8, 128))
    product = 2 * half * labels * width
    g_own = pl.pallas_call(
        own_kernel,
        out_shape=jax.ShapeDtypeStruct((half, labels), BF),
        in_specs=[vmem] * 3,
        out_specs=vmem,
        scratch_shapes=half_scratch,
        compiler_params=pltpu.CompilerParams(vmem_limit_bytes=16 * MIB),
        cost_estimate=pl.CostEstimate(
            flops=product, bytes_accessed=2 * labels * width, transcendentals=2 * half * labels),
        name="own_label_grad",
    )(own, staged, label_bias)
    g, g_other, theirs = pl.pallas_call(
        other_kernel,
        out_shape=(
            jax.ShapeDtypeStruct((8, half, labels), BF),
            jax.ShapeDtypeStruct((half, labels), BF),
            blocks_of(BF),
        ),
        in_specs=[vmem] * 5,
        out_specs=(hbm, vmem, vmem),
        scratch_shapes=[dx_scratch] + half_scratch + [pltpu.SemaphoreType.DMA((3,))],
        compiler_params=pltpu.CompilerParams(vmem_limit_bytes=OTHER_VMEM),
        cost_estimate=pl.CostEstimate(
            flops=2 * product, bytes_accessed=2 * labels * width, transcendentals=2 * half * labels),
        name="other_label_grad",
    )(own, other, g_own, staged, label_bias)
    received = xor_permute(theirs, "c", 2, 1)
    mine, g = pl.pallas_call(
        own_dx_kernel,
        out_shape=(blocks_of(F32), jax.ShapeDtypeStruct(g.shape, BF)),
        in_specs=[vmem] * 3 + [hbm],
        out_specs=(vmem, hbm),
        input_output_aliases={3: 1},
        scratch_shapes=[dx_scratch, pltpu.SemaphoreType.DMA],
        compiler_params=pltpu.CompilerParams(vmem_limit_bytes=OTHER_VMEM),
        cost_estimate=pl.CostEstimate(flops=product, bytes_accessed=2 * labels * width, transcendentals=0),
        name="own_dx",
    )(g_own, staged, g_other, g)
    send = pl.pallas_call(
        join_kernel,
        out_shape=blocks_of(BF),
        in_specs=[vmem] * 2,
        out_specs=vmem,
        compiler_params=pltpu.CompilerParams(vmem_limit_bytes=16 * MIB),
        name="join",
    )(mine, received)
    send, g = lax.optimization_barrier((send, g))
    parts = lax.all_to_all(send, ("zh", "x", "zl", "y"), 0, 0)

    weight_grad, bias_grad = pl.pallas_call(
        weight_kernel,
        out_shape=(jax.ShapeDtypeStruct((labels, width), BF), jax.ShapeDtypeStruct((labels,), F32)),
        in_specs=[hbm],
        out_specs=(hbm, hbm),
        scratch_shapes=[
            pltpu.VMEM((rows, labels), BF),
            pltpu.VMEM((rows, width), BF),
            pltpu.VMEM((labels, width), BF),
            pltpu.VMEM((labels,), F32),
            pltpu.SemaphoreType.DMA((2 * n_chunks,)),
            pltpu.SemaphoreType.DMA((n_chunks,)),
            pltpu.SemaphoreType.DMA((2,)),
            pltpu.SemaphoreType.DMA,
        ],
        compiler_params=pltpu.CompilerParams(vmem_limit_bytes=WEIGHT_VMEM),
        cost_estimate=pl.CostEstimate(
            flops=2 * rows * labels * width, bytes_accessed=2 * labels * (width + rows), transcendentals=0),
        name="weight_grad",
    )(g)
    feature_grad = pl.pallas_call(
        total_kernel,
        out_shape=jax.ShapeDtypeStruct((per, 64), BF),
        in_specs=[vmem],
        out_specs=vmem,
        compiler_params=pltpu.CompilerParams(vmem_limit_bytes=16 * MIB),
        name="total",
    )(parts)
    return weight_grad, bias_grad, feature_grad


def solution(mesh):
    fine = Mesh(mesh.devices.reshape(2, 4, 4, 4, 2), ("zh", "x", "zl", "y", "c"))
    row, col = ("zh", "x"), ("zl", "y", "c")
    return jax.shard_map(
        local,
        mesh=fine,
        in_specs=(P(col, None), P(row + col, None), P(row + col), P(col, None), P(col)),
        out_specs=(P(row + col, None), P(row + col), P(col, row)),
        check_vma=False,
    )
```

```python
import functools

import jax
import jax.numpy as jnp
import numpy as np
from jax import lax
from jax.experimental import pallas as pl
from jax.experimental.pallas import tpu as pltpu
from jax.sharding import Mesh, PartitionSpec as P

BF = jnp.bfloat16
F32 = jnp.float32
KEY = 8192
BITS = (0, 3, 2, 1)
CHUNK = 1024
DX_CHUNK = 2048
ROWS_AT_ONCE = 64
MIB = 1024 * 1024
WEIGHT_VMEM = 50 * MIB
OTHER_VMEM = 38 * MIB


def cuts(total, size):
    return [(a, min(size, total - a)) for a in range(0, total, size)]


def xor_permute(x, axis, size, bit):
    return lax.ppermute(x, axis, [(i, i ^ bit) for i in range(size)])


def pack_kernel(*refs):
    *parts, out_ref = refs
    n = parts[0].shape[0]
    for i, part in enumerate(parts):
        out_ref[i * n:(i + 1) * n] = part[...]


def stage_kernel(w_hbm, w_ref, sem):
    copy = pltpu.make_async_copy(w_hbm, w_ref, sem)
    copy.start()
    copy.wait()


def half_grad(rows_ref, w_ref, bias_ref, g_ref, first_scr, key_scr, even_scr, odd_scr):
    labels, width = w_ref.shape
    half = rows_ref.shape[0]
    chunks = cuts(labels, CHUNK)
    zh, x, zl, y, c = (lax.axis_index(a) for a in ("zh", "x", "zl", "y", "c"))
    offset = ((((zh * 4 + x) * 4 + zl) * 4 + y) * 2 + c) * labels

    digit = lax.broadcasted_iota(jnp.int32, (128, 128), 0)
    lane = lax.broadcasted_iota(jnp.int32, (128, 128), 1)
    same = (digit % 32) == (lane % 32)
    power = jnp.where(digit < 32, 1.0, jnp.where(digit < 64, 256.0, jnp.where(digit < 96, 65536.0, 0.0)))
    decode = jnp.where(same, power, 0.0).astype(BF)
    row = lax.broadcasted_iota(jnp.int32, (half, 128), 0).astype(F32)
    local = jnp.dot(rows_ref[:, width:width + 128], decode, preferred_element_type=F32) - offset.astype(F32)
    local = jnp.where((local >= 0.0) & (local < float(labels)), local, -1.0)
    first = jnp.max(local, axis=1, keepdims=True)
    first_scr[...] = jnp.broadcast_to(first, (half, 128))
    more = (local >= 0.0) & (local < first)
    key_scr[...] = jnp.where(more, row * float(KEY) + local, -1.0)

    buffers = (even_scr, odd_scr)
    lanes = lax.broadcasted_iota(jnp.int32, (ROWS_AT_ONCE, 128), 1).astype(F32)

    def logits(i):
        a, n = chunks[i]
        buffers[i % 2][:, 0:n] = lax.dot_general(
            rows_ref[:, 0:width], w_ref[a:a + n], (((1,), (1,)), ((), ())), preferred_element_type=F32)

    logits(0)
    for i, (a, n) in enumerate(chunks):
        if i + 1 < len(chunks):
            logits(i + 1)
        for k in range(0, n, 128):
            bias = bias_ref[a + k:a + k + 128].reshape(1, 128)
            for r in range(0, half, ROWS_AT_ONCE):
                x = buffers[i % 2][r:r + ROWS_AT_ONCE, k:k + 128] + bias
                s = pltpu.reciprocal(1.0 + jnp.exp(-x), approx=True)
                hit = (first_scr[r:r + ROWS_AT_ONCE] - float(a + k)) == lanes
                g_ref[r:r + ROWS_AT_ONCE, a + k:a + k + 128] = jnp.where(hit, s - 1.0, s).astype(BF)

    def one_hit(top):
        key = top.astype(jnp.int32)
        b = key // KEY
        l = key - b * KEY
        b16 = pl.ds(pl.multiple_of((b // 16) * 16, 16), 16)
        l128 = pl.ds(pl.multiple_of((l // 128) * 128, 128), 128)
        r = lax.broadcasted_iota(jnp.int32, (16, 128), 0)
        c = lax.broadcasted_iota(jnp.int32, (16, 128), 1)
        old = g_ref[b16, l128].astype(F32)
        g_ref[b16, l128] = jnp.where((r == b % 16) & (c == l % 128), old - 1.0, old).astype(BF)
        keys = key_scr[...]
        keys = jnp.where(keys == top, -1.0, keys)
        key_scr[...] = keys
        return jnp.max(keys)

    lax.while_loop(lambda top: top >= 0.0, one_hit, jnp.max(key_scr[...]))


def half_dx(g_ref, w_ref, dx_scr, out_ref):
    labels, width = w_ref.shape
    half = g_ref.shape[0]
    for j, (a, n) in enumerate(cuts(labels, DX_CHUNK)):
        term = jnp.dot(g_ref[:, a:a + n], w_ref[a:a + n], preferred_element_type=F32)
        if j == 0:
            dx_scr[0:half] = term
        else:
            dx_scr[0:half] += term
    dx_scr[half:half + 16] = jnp.zeros((16, width), F32)
    zl, y = lax.axis_index("zl"), lax.axis_index("y")
    low = lax.broadcasted_iota(jnp.int32, (8, 128), 1) < 64
    per = half // 16
    for k in range(width // 128):
        here = dx_scr[:, k * 128:(k + 1) * 128]
        turned = pltpu.roll(here, 64, 1)
        for pz, jz in enumerate(BITS):
            for py, jy in enumerate(BITS):
                j = (pz * 4 + py) * per
                to_chip = (zl ^ jz) * 4 + (y ^ jy)
                m = j + per // 2
                even = jnp.where(low, here[j:j + 8], turned[m:m + 8])
                odd = jnp.where(low, turned[j:j + 8], here[m:m + 8])
                out_ref[32 * k + to_chip] = even.astype(out_ref.dtype)
                out_ref[32 * k + 16 + to_chip] = odd.astype(out_ref.dtype)


def own_kernel(own_ref, w_ref, bias_ref, g_ref, *scratch):
    half_grad(own_ref, w_ref, bias_ref, g_ref, *scratch)


def other_kernel(own_ref, other_ref, g_own_ref, w_ref, bias_ref, g_hbm, g_ref, theirs_ref, dx_scr, first_scr, key_scr, even_scr, odd_scr, sems):
    width = w_ref.shape[1]
    cols = pl.ds(0, width)
    early = [
        pltpu.make_async_copy(g_own_ref, g_hbm.at[0], sems.at[0]),
        pltpu.make_async_copy(own_ref.at[:, cols], g_hbm.at[1, :, cols], sems.at[1]),
        pltpu.make_async_copy(other_ref.at[:, cols], g_hbm.at[2, :, cols], sems.at[2]),
    ]
    for copy in early:
        copy.start()
    half_grad(other_ref, w_ref, bias_ref, g_ref, first_scr, key_scr, even_scr, odd_scr)
    half_dx(g_ref, w_ref, dx_scr, theirs_ref)
    for copy in early:
        copy.wait()


def own_dx_kernel(g_ref, w_ref, mine_ref, dx_scr):
    half_dx(g_ref, w_ref, dx_scr, mine_ref)


def join_kernel(mine_ref, received_ref, out_ref):
    out_ref[...] = (mine_ref[...] + received_ref[...].astype(F32)).astype(BF)


def total_kernel(parts_ref, out_ref):
    total = jnp.sum(parts_ref[...].astype(F32), axis=0)
    per, cols = out_ref.shape
    total = total[0:per // 2]
    out_ref[...] = jnp.concatenate([total[:, 0:cols], total[:, cols:2 * cols]], axis=0).astype(BF)


def weight_kernel(g_hbm, g_other_hbm, wg_hbm, bg_hbm, g_scr, f_scr, out_scr, bias_scr, g_sems, out_sems, f_sems, bias_sem):
    labels, width = wg_hbm.shape
    chunks = cuts(labels, CHUNK)
    half = g_hbm.shape[1]
    halves = [pl.ds(0, half), pl.ds(half, half)]
    f_copies = [
        pltpu.make_async_copy(g_hbm.at[1 + h, :, pl.ds(0, width)], f_scr.at[at], f_sems.at[h])
        for h, at in enumerate(halves)
    ]
    g_copies = [
        pltpu.make_async_copy(from_ref.at[:, pl.ds(a, n)], g_scr.at[at, pl.ds(a, n)], g_sems.at[2 * i + h])
        for i, (a, n) in enumerate(chunks)
        for h, (at, from_ref) in enumerate(zip(halves, (g_hbm.at[0], g_other_hbm)))
    ]
    out_copies = [
        pltpu.make_async_copy(out_scr.at[pl.ds(a, n)], wg_hbm.at[pl.ds(a, n)], out_sems.at[i])
        for i, (a, n) in enumerate(chunks)
    ]
    for copy in f_copies + g_copies:
        copy.start()
    for copy in f_copies:
        copy.wait()
    for i, (a, n) in enumerate(chunks):
        g_copies[2 * i].wait()
        g_copies[2 * i + 1].wait()
        g = g_scr[:, a:a + n]
        out_scr[a:a + n] = lax.dot_general(
            g, f_scr[...], (((0,), (0,)), ((), ())), preferred_element_type=F32).astype(BF)
        out_copies[i].start()
        bias_scr[a:a + n] = jnp.sum(g.astype(F32), axis=0)
    bias_copy = pltpu.make_async_copy(bias_scr, bg_hbm, bias_sem)
    bias_copy.start()
    for copy in out_copies + [bias_copy]:
        copy.wait()


def local(features, weights, label_bias, pos_ids, pos_count):
    labels, width = weights.shape
    per, slots = pos_ids.shape
    half = per * 16
    rows = 2 * half
    wide = width + 4 * slots
    vmem = pl.BlockSpec(memory_space=pltpu.VMEM)
    hbm = pl.BlockSpec(memory_space=pltpu.HBM)
    n_chunks = len(cuts(labels, CHUNK))

    lane = np.arange(wide) - width
    slot = np.where(lane < 0, 0, lane % slots).astype(np.int32)
    shift = (8 * np.clip(lane // slots, 0, 2)).astype(np.int32)
    ids = sum(
        jnp.pad(pos_ids, ((0, 0), (width + k * slots, (3 - k) * slots))) for k in range(3))
    ids = jnp.where(slot[None, :] < pos_count[:, None], ids, 0xFFFFFF)
    digits = lax.shift_right_logical(ids, jnp.broadcast_to(shift[None, :], ids.shape)) & 255
    pay = jnp.where(
        (lane < 0)[None, :], jnp.pad(features, ((0, 0), (0, wide - width))), digits.astype(BF))
    pay = jnp.concatenate([pay] + [xor_permute(pay, "y", 4, d) for d in BITS[1:]], axis=0)
    pay, weights_then = lax.optimization_barrier((pay, weights))
    staged = pl.pallas_call(
        stage_kernel,
        out_shape=jax.ShapeDtypeStruct((labels, width), BF),
        in_specs=[hbm],
        out_specs=vmem,
        scratch_shapes=[pltpu.SemaphoreType.DMA],
        compiler_params=pltpu.CompilerParams(vmem_limit_bytes=46 * MIB),
        cost_estimate=pl.CostEstimate(flops=0, bytes_accessed=4 * labels * width, transcendentals=0),
        name="stage_weights",
    )(weights_then)
    zs = [xor_permute(pay, "zl", 4, d) for d in BITS[1:]]
    staged, *zs = lax.optimization_barrier((staged, *zs))
    own = pl.pallas_call(
        pack_kernel,
        out_shape=jax.ShapeDtypeStruct((half, wide), BF),
        in_specs=[vmem] * 4,
        out_specs=vmem,
        compiler_params=pltpu.CompilerParams(vmem_limit_bytes=4 * MIB),
        name="pack",
    )(pay, *zs)
    other = xor_permute(own, "c", 2, 1)

    half_scratch = [
        pltpu.VMEM((half, 128), F32),
        pltpu.VMEM((half, 128), F32),
        pltpu.VMEM((half, CHUNK), F32),
        pltpu.VMEM((half, CHUNK), F32),
    ]
    dx_scratch = pltpu.VMEM((half + 16, width), F32)
    blocks_of = functools.partial(jax.ShapeDtypeStruct, (128, 8, 128))
    product = 2 * half * labels * width
    g_own = pl.pallas_call(
        own_kernel,
        out_shape=jax.ShapeDtypeStruct((half, labels), BF),
        in_specs=[vmem] * 3,
        out_specs=vmem,
        scratch_shapes=half_scratch,
        compiler_params=pltpu.CompilerParams(vmem_limit_bytes=16 * MIB),
        cost_estimate=pl.CostEstimate(
            flops=product, bytes_accessed=2 * labels * width, transcendentals=2 * half * labels),
        name="own_label_grad",
    )(own, staged, label_bias)
    g, g_other, theirs = pl.pallas_call(
        other_kernel,
        out_shape=(
            jax.ShapeDtypeStruct((8, half, labels), BF),
            jax.ShapeDtypeStruct((half, labels), BF),
            blocks_of(BF),
        ),
        in_specs=[vmem] * 5,
        out_specs=(hbm, vmem, vmem),
        scratch_shapes=[dx_scratch] + half_scratch + [pltpu.SemaphoreType.DMA((3,))],
        compiler_params=pltpu.CompilerParams(vmem_limit_bytes=OTHER_VMEM),
        cost_estimate=pl.CostEstimate(
            flops=2 * product, bytes_accessed=2 * labels * width, transcendentals=2 * half * labels),
        name="other_label_grad",
    )(own, other, g_own, staged, label_bias)
    received = xor_permute(theirs, "c", 2, 1)
    mine = pl.pallas_call(
        own_dx_kernel,
        out_shape=blocks_of(F32),
        in_specs=[vmem] * 2,
        out_specs=vmem,
        scratch_shapes=[dx_scratch],
        compiler_params=pltpu.CompilerParams(vmem_limit_bytes=OTHER_VMEM),
        cost_estimate=pl.CostEstimate(flops=product, bytes_accessed=2 * labels * width, transcendentals=0),
        name="own_dx",
    )(g_own, staged)
    send = pl.pallas_call(
        join_kernel,
        out_shape=blocks_of(BF),
        in_specs=[vmem] * 2,
        out_specs=vmem,
        compiler_params=pltpu.CompilerParams(vmem_limit_bytes=16 * MIB),
        name="join",
    )(mine, received)
    send, g, g_other = lax.optimization_barrier((send, g, g_other))
    parts = lax.all_to_all(send, ("zh", "x", "zl", "y"), 0, 0)

    weight_grad, bias_grad = pl.pallas_call(
        weight_kernel,
        out_shape=(jax.ShapeDtypeStruct((labels, width), BF), jax.ShapeDtypeStruct((labels,), F32)),
        in_specs=[hbm, hbm],
        out_specs=(hbm, hbm),
        scratch_shapes=[
            pltpu.VMEM((rows, labels), BF),
            pltpu.VMEM((rows, width), BF),
            pltpu.VMEM((labels, width), BF),
            pltpu.VMEM((labels,), F32),
            pltpu.SemaphoreType.DMA((2 * n_chunks,)),
            pltpu.SemaphoreType.DMA((n_chunks,)),
            pltpu.SemaphoreType.DMA((2,)),
            pltpu.SemaphoreType.DMA,
        ],
        compiler_params=pltpu.CompilerParams(vmem_limit_bytes=WEIGHT_VMEM),
        cost_estimate=pl.CostEstimate(
            flops=2 * rows * labels * width, bytes_accessed=2 * labels * (width + rows), transcendentals=0),
        name="weight_grad",
    )(g, g_other)
    feature_grad = pl.pallas_call(
        total_kernel,
        out_shape=jax.ShapeDtypeStruct((per, 64), BF),
        in_specs=[vmem],
        out_specs=vmem,
        compiler_params=pltpu.CompilerParams(vmem_limit_bytes=16 * MIB),
        name="total",
    )(parts)
    return weight_grad, bias_grad, feature_grad


def solution(mesh):
    fine = Mesh(mesh.devices.reshape(2, 4, 4, 4, 2), ("zh", "x", "zl", "y", "c"))
    row, col = ("zh", "x"), ("zl", "y", "c")
    return jax.shard_map(
        local,
        mesh=fine,
        in_specs=(P(col, None), P(row + col, None), P(row + col), P(col, None), P(col)),
        out_specs=(P(row + col, None), P(row + col), P(col, row)),
        check_vma=False,
    )
```

```python
import functools

import jax
import jax.numpy as jnp
import numpy as np
from jax import lax
from jax.experimental import pallas as pl
from jax.experimental.pallas import tpu as pltpu
from jax.sharding import Mesh, PartitionSpec as P

BF = jnp.bfloat16
F32 = jnp.float32
KEY = 8192
BITS = (0, 3, 2, 1)
CHUNK = 1024
DX_CHUNK = 2048
ROWS_AT_ONCE = 64
MIB = 1024 * 1024
WEIGHT_VMEM = 50 * MIB
OTHER_VMEM = 38 * MIB


def cuts(total, size):
    return [(a, min(size, total - a)) for a in range(0, total, size)]


def xor_permute(x, axis, size, bit):
    return lax.ppermute(x, axis, [(i, i ^ bit) for i in range(size)])


def pack_kernel(*refs):
    *parts, out_ref = refs
    n = parts[0].shape[0]
    for i, part in enumerate(parts):
        out_ref[i * n:(i + 1) * n] = part[...]


def stage_kernel(w_hbm, w_ref, sem):
    copy = pltpu.make_async_copy(w_hbm, w_ref, sem)
    copy.start()
    copy.wait()


def half_grad(rows_ref, w_ref, bias_ref, g_ref, first_scr, key_scr, even_scr, odd_scr, dx_scr=None):
    labels, width = w_ref.shape
    half = rows_ref.shape[0]
    chunks = cuts(labels, CHUNK)
    zh, x, zl, y, c = (lax.axis_index(a) for a in ("zh", "x", "zl", "y", "c"))
    offset = ((((zh * 4 + x) * 4 + zl) * 4 + y) * 2 + c) * labels

    digit = lax.broadcasted_iota(jnp.int32, (128, 128), 0)
    lane = lax.broadcasted_iota(jnp.int32, (128, 128), 1)
    same = (digit % 32) == (lane % 32)
    power = jnp.where(digit < 32, 1.0, jnp.where(digit < 64, 256.0, jnp.where(digit < 96, 65536.0, 0.0)))
    decode = jnp.where(same, power, 0.0).astype(BF)
    row = lax.broadcasted_iota(jnp.int32, (half, 128), 0).astype(F32)
    local = jnp.dot(rows_ref[:, width:width + 128], decode, preferred_element_type=F32) - offset.astype(F32)
    local = jnp.where((local >= 0.0) & (local < float(labels)), local, -1.0)
    first = jnp.max(local, axis=1, keepdims=True)
    first_scr[...] = jnp.broadcast_to(first, (half, 128))
    more = (local >= 0.0) & (local < first)
    key_scr[...] = jnp.where(more, row * float(KEY) + local, -1.0)

    buffers = (even_scr, odd_scr)
    lanes = lax.broadcasted_iota(jnp.int32, (ROWS_AT_ONCE, 128), 1).astype(F32)

    def logits(i):
        a, n = chunks[i]
        buffers[i % 2][:, 0:n] = lax.dot_general(
            rows_ref[:, 0:width], w_ref[a:a + n], (((1,), (1,)), ((), ())), preferred_element_type=F32)

    def add_dx(i):
        a, n = chunks[i]
        term = jnp.dot(g_ref[:, a:a + n], w_ref[a:a + n], preferred_element_type=F32)
        if i == 0:
            dx_scr[0:half] = term
        else:
            dx_scr[0:half] += term

    logits(0)
    for i, (a, n) in enumerate(chunks):
        if i + 1 < len(chunks):
            logits(i + 1)
        if dx_scr is not None and i > 0:
            add_dx(i - 1)
        for k in range(0, n, 128):
            bias = bias_ref[a + k:a + k + 128].reshape(1, 128)
            for r in range(0, half, ROWS_AT_ONCE):
                x = buffers[i % 2][r:r + ROWS_AT_ONCE, k:k + 128] + bias
                s = pltpu.reciprocal(1.0 + jnp.exp(-x), approx=True)
                hit = (first_scr[r:r + ROWS_AT_ONCE] - float(a + k)) == lanes
                g_ref[r:r + ROWS_AT_ONCE, a + k:a + k + 128] = jnp.where(hit, s - 1.0, s).astype(BF)

    if dx_scr is not None:
        add_dx(len(chunks) - 1)

    def one_hit(top):
        key = top.astype(jnp.int32)
        b = key // KEY
        l = key - b * KEY
        b16 = pl.ds(pl.multiple_of((b // 16) * 16, 16), 16)
        l128 = pl.ds(pl.multiple_of((l // 128) * 128, 128), 128)
        r = lax.broadcasted_iota(jnp.int32, (16, 128), 0)
        c = lax.broadcasted_iota(jnp.int32, (16, 128), 1)
        old = g_ref[b16, l128].astype(F32)
        g_ref[b16, l128] = jnp.where((r == b % 16) & (c == l % 128), old - 1.0, old).astype(BF)
        if dx_scr is not None:
            l16 = pl.ds(pl.multiple_of((l // 16) * 16, 16), 16)
            r = lax.broadcasted_iota(jnp.int32, (16, width), 0)
            w_row = jnp.sum(jnp.where(r == l % 16, w_ref[l16].astype(F32), 0.0), axis=0, keepdims=True)
            dx_scr[b16] -= jnp.where(r == b % 16, w_row, 0.0)
        keys = key_scr[...]
        keys = jnp.where(keys == top, -1.0, keys)
        key_scr[...] = keys
        return jnp.max(keys)

    lax.while_loop(lambda top: top >= 0.0, one_hit, jnp.max(key_scr[...]))


def half_dx(g_ref, w_ref, dx_scr, out_ref, with_product=True):
    labels, width = w_ref.shape
    half = g_ref.shape[0]
    for j, (a, n) in enumerate(cuts(labels, DX_CHUNK) if with_product else []):
        term = jnp.dot(g_ref[:, a:a + n], w_ref[a:a + n], preferred_element_type=F32)
        if j == 0:
            dx_scr[0:half] = term
        else:
            dx_scr[0:half] += term
    dx_scr[half:half + 16] = jnp.zeros((16, width), F32)
    zl, y = lax.axis_index("zl"), lax.axis_index("y")
    low = lax.broadcasted_iota(jnp.int32, (8, 128), 1) < 64
    per = half // 16
    for k in range(width // 128):
        here = dx_scr[:, k * 128:(k + 1) * 128]
        turned = pltpu.roll(here, 64, 1)
        for pz, jz in enumerate(BITS):
            for py, jy in enumerate(BITS):
                j = (pz * 4 + py) * per
                to_chip = (zl ^ jz) * 4 + (y ^ jy)
                m = j + per // 2
                even = jnp.where(low, here[j:j + 8], turned[m:m + 8])
                odd = jnp.where(low, turned[j:j + 8], here[m:m + 8])
                out_ref[32 * k + to_chip] = even.astype(out_ref.dtype)
                out_ref[32 * k + 16 + to_chip] = odd.astype(out_ref.dtype)


def own_kernel(own_ref, w_ref, bias_ref, g_ref, *scratch):
    half_grad(own_ref, w_ref, bias_ref, g_ref, *scratch)


def other_kernel(own_ref, other_ref, g_own_ref, w_ref, bias_ref, g_hbm, g_ref, theirs_ref, dx_scr, first_scr, key_scr, even_scr, odd_scr, sems):
    width = w_ref.shape[1]
    cols = pl.ds(0, width)
    early = [
        pltpu.make_async_copy(g_own_ref, g_hbm.at[0], sems.at[0]),
        pltpu.make_async_copy(own_ref.at[:, cols], g_hbm.at[1, :, cols], sems.at[1]),
        pltpu.make_async_copy(other_ref.at[:, cols], g_hbm.at[2, :, cols], sems.at[2]),
    ]
    for copy in early:
        copy.start()
    half_grad(other_ref, w_ref, bias_ref, g_ref, first_scr, key_scr, even_scr, odd_scr, dx_scr)
    half_dx(g_ref, w_ref, dx_scr, theirs_ref, with_product=False)
    for copy in early:
        copy.wait()


def own_dx_kernel(g_ref, w_ref, mine_ref, dx_scr):
    half_dx(g_ref, w_ref, dx_scr, mine_ref)


def join_kernel(mine_ref, received_ref, out_ref):
    out_ref[...] = (mine_ref[...] + received_ref[...].astype(F32)).astype(BF)


def total_kernel(parts_ref, out_ref):
    total = jnp.sum(parts_ref[...].astype(F32), axis=0)
    per, cols = out_ref.shape
    total = total[0:per // 2]
    out_ref[...] = jnp.concatenate([total[:, 0:cols], total[:, cols:2 * cols]], axis=0).astype(BF)


def weight_kernel(g_hbm, g_other_hbm, wg_hbm, bg_hbm, g_scr, f_scr, out_scr, bias_scr, g_sems, out_sems, f_sems, bias_sem):
    labels, width = wg_hbm.shape
    chunks = cuts(labels, CHUNK)
    half = g_hbm.shape[1]
    halves = [pl.ds(0, half), pl.ds(half, half)]
    f_copies = [
        pltpu.make_async_copy(g_hbm.at[1 + h, :, pl.ds(0, width)], f_scr.at[at], f_sems.at[h])
        for h, at in enumerate(halves)
    ]
    g_copies = [
        pltpu.make_async_copy(from_ref.at[:, pl.ds(a, n)], g_scr.at[at, pl.ds(a, n)], g_sems.at[2 * i + h])
        for i, (a, n) in enumerate(chunks)
        for h, (at, from_ref) in enumerate(zip(halves, (g_hbm.at[0], g_other_hbm)))
    ]
    out_copies = [
        pltpu.make_async_copy(out_scr.at[pl.ds(a, n)], wg_hbm.at[pl.ds(a, n)], out_sems.at[i])
        for i, (a, n) in enumerate(chunks)
    ]
    for copy in f_copies + g_copies:
        copy.start()
    for copy in f_copies:
        copy.wait()
    for i, (a, n) in enumerate(chunks):
        g_copies[2 * i].wait()
        g_copies[2 * i + 1].wait()
        g = g_scr[:, a:a + n]
        out_scr[a:a + n] = lax.dot_general(
            g, f_scr[...], (((0,), (0,)), ((), ())), preferred_element_type=F32).astype(BF)
        out_copies[i].start()
        bias_scr[a:a + n] = jnp.sum(g.astype(F32), axis=0)
    bias_copy = pltpu.make_async_copy(bias_scr, bg_hbm, bias_sem)
    bias_copy.start()
    for copy in out_copies + [bias_copy]:
        copy.wait()


def local(features, weights, label_bias, pos_ids, pos_count):
    labels, width = weights.shape
    per, slots = pos_ids.shape
    half = per * 16
    rows = 2 * half
    wide = width + 4 * slots
    vmem = pl.BlockSpec(memory_space=pltpu.VMEM)
    hbm = pl.BlockSpec(memory_space=pltpu.HBM)
    n_chunks = len(cuts(labels, CHUNK))

    lane = np.arange(wide) - width
    slot = np.where(lane < 0, 0, lane % slots).astype(np.int32)
    shift = (8 * np.clip(lane // slots, 0, 2)).astype(np.int32)
    ids = sum(
        jnp.pad(pos_ids, ((0, 0), (width + k * slots, (3 - k) * slots))) for k in range(3))
    ids = jnp.where(slot[None, :] < pos_count[:, None], ids, 0xFFFFFF)
    digits = lax.shift_right_logical(ids, jnp.broadcast_to(shift[None, :], ids.shape)) & 255
    pay = jnp.where(
        (lane < 0)[None, :], jnp.pad(features, ((0, 0), (0, wide - width))), digits.astype(BF))
    pay = jnp.concatenate([pay] + [xor_permute(pay, "y", 4, d) for d in BITS[1:]], axis=0)
    pay, weights_then = lax.optimization_barrier((pay, weights))
    staged = pl.pallas_call(
        stage_kernel,
        out_shape=jax.ShapeDtypeStruct((labels, width), BF),
        in_specs=[hbm],
        out_specs=vmem,
        scratch_shapes=[pltpu.SemaphoreType.DMA],
        compiler_params=pltpu.CompilerParams(vmem_limit_bytes=46 * MIB),
        cost_estimate=pl.CostEstimate(flops=0, bytes_accessed=4 * labels * width, transcendentals=0),
        name="stage_weights",
    )(weights_then)
    zs = [xor_permute(pay, "zl", 4, d) for d in BITS[1:]]
    staged, *zs = lax.optimization_barrier((staged, *zs))
    own = pl.pallas_call(
        pack_kernel,
        out_shape=jax.ShapeDtypeStruct((half, wide), BF),
        in_specs=[vmem] * 4,
        out_specs=vmem,
        compiler_params=pltpu.CompilerParams(vmem_limit_bytes=4 * MIB),
        name="pack",
    )(pay, *zs)
    other = xor_permute(own, "c", 2, 1)

    half_scratch = [
        pltpu.VMEM((half, 128), F32),
        pltpu.VMEM((half, 128), F32),
        pltpu.VMEM((half, CHUNK), F32),
        pltpu.VMEM((half, CHUNK), F32),
    ]
    dx_scratch = pltpu.VMEM((half + 16, width), F32)
    blocks_of = functools.partial(jax.ShapeDtypeStruct, (128, 8, 128))
    product = 2 * half * labels * width
    g_own = pl.pallas_call(
        own_kernel,
        out_shape=jax.ShapeDtypeStruct((half, labels), BF),
        in_specs=[vmem] * 3,
        out_specs=vmem,
        scratch_shapes=half_scratch,
        compiler_params=pltpu.CompilerParams(vmem_limit_bytes=16 * MIB),
        cost_estimate=pl.CostEstimate(
            flops=product, bytes_accessed=2 * labels * width, transcendentals=2 * half * labels),
        name="own_label_grad",
    )(own, staged, label_bias)
    g, g_other, theirs = pl.pallas_call(
        other_kernel,
        out_shape=(
            jax.ShapeDtypeStruct((8, half, labels), BF),
            jax.ShapeDtypeStruct((half, labels), BF),
            blocks_of(BF),
        ),
        in_specs=[vmem] * 5,
        out_specs=(hbm, vmem, vmem),
        scratch_shapes=[dx_scratch] + half_scratch + [pltpu.SemaphoreType.DMA((3,))],
        compiler_params=pltpu.CompilerParams(vmem_limit_bytes=OTHER_VMEM),
        cost_estimate=pl.CostEstimate(
            flops=2 * product, bytes_accessed=2 * labels * width, transcendentals=2 * half * labels),
        name="other_label_grad",
    )(own, other, g_own, staged, label_bias)
    received = xor_permute(theirs, "c", 2, 1)
    mine = pl.pallas_call(
        own_dx_kernel,
        out_shape=blocks_of(F32),
        in_specs=[vmem] * 2,
        out_specs=vmem,
        scratch_shapes=[dx_scratch],
        compiler_params=pltpu.CompilerParams(vmem_limit_bytes=OTHER_VMEM),
        cost_estimate=pl.CostEstimate(flops=product, bytes_accessed=2 * labels * width, transcendentals=0),
        name="own_dx",
    )(g_own, staged)
    send = pl.pallas_call(
        join_kernel,
        out_shape=blocks_of(BF),
        in_specs=[vmem] * 2,
        out_specs=vmem,
        compiler_params=pltpu.CompilerParams(vmem_limit_bytes=16 * MIB),
        name="join",
    )(mine, received)
    send, g, g_other = lax.optimization_barrier((send, g, g_other))
    parts = lax.all_to_all(send, ("zh", "x", "zl", "y"), 0, 0)

    weight_grad, bias_grad = pl.pallas_call(
        weight_kernel,
        out_shape=(jax.ShapeDtypeStruct((labels, width), BF), jax.ShapeDtypeStruct((labels,), F32)),
        in_specs=[hbm, hbm],
        out_specs=(hbm, hbm),
        scratch_shapes=[
            pltpu.VMEM((rows, labels), BF),
            pltpu.VMEM((rows, width), BF),
            pltpu.VMEM((labels, width), BF),
            pltpu.VMEM((labels,), F32),
            pltpu.SemaphoreType.DMA((2 * n_chunks,)),
            pltpu.SemaphoreType.DMA((n_chunks,)),
            pltpu.SemaphoreType.DMA((2,)),
            pltpu.SemaphoreType.DMA,
        ],
        compiler_params=pltpu.CompilerParams(vmem_limit_bytes=WEIGHT_VMEM),
        cost_estimate=pl.CostEstimate(
            flops=2 * rows * labels * width, bytes_accessed=2 * labels * (width + rows), transcendentals=0),
        name="weight_grad",
    )(g, g_other)
    feature_grad = pl.pallas_call(
        total_kernel,
        out_shape=jax.ShapeDtypeStruct((per, 64), BF),
        in_specs=[vmem],
        out_specs=vmem,
        compiler_params=pltpu.CompilerParams(vmem_limit_bytes=16 * MIB),
        name="total",
    )(parts)
    return weight_grad, bias_grad, feature_grad


def solution(mesh):
    fine = Mesh(mesh.devices.reshape(2, 4, 4, 4, 2), ("zh", "x", "zl", "y", "c"))
    row, col = ("zh", "x"), ("zl", "y", "c")
    return jax.shard_map(
        local,
        mesh=fine,
        in_specs=(P(col, None), P(row + col, None), P(row + col), P(col, None), P(col)),
        out_specs=(P(row + col, None), P(row + col), P(col, row)),
        check_vma=False,
    )
```
